32 devices in a mesh: dp: 4 (over y, x), row: 4 (over z), col: 2 (over core).
Axes of the slice: x: 2, y: 2, z: 4, core: 2. Of those that a mesh axis runs over, the one named last changes fastest.
Arguments:
- tokens: bfloat16 [1024, 4096], P(('dp', 'col'), 'row'), may hold values from -6 to 6
- w_up: bfloat16 [4096, 16384], P('row', 'col'), may hold values from -0.09375 to 0.09375
- w_down: bfloat16 [4096, 16384], P('row', 'col'), may hold values from -0.046875 to 0.046875
- cotangent: bfloat16 [1024, 4096], P(('dp', 'col'), 'row'), may hold values from -6 to 6
Outputs:
- output: bfloat16 [1024, 4096], P(('dp', 'col'), 'row')
- input_grad: bfloat16 [1024, 4096], P(('dp', 'col'), 'row')
- up_grad: float32 [4096, 16384], P('row', ('col', 'dp'))
- down_grad: float32 [4096, 16384], P('row', ('col', 'dp'))
The draws below stay inside these ranges and needn't reach their ends.
All inputs are finite; a program needn't handle non-finite values.
Results may differ from the reference program's by a relative error of at most 0.018.
Values may be sent and summed in bfloat16 or wider, within the bound.
No kernel may reach another device: no remote copies, remote signals or barrier semaphores. Data moves between devices by JAX's collectives and lax.ppermute only.
A program may use at most 192 MiB of HBM per device.

```python
import jax
import jax.numpy as jnp
from jax import lax

D = 4096
F = 16384
TOKENS = 1024
N_ROW = 4


def block_scale(own_key, shape, pieces, smallest, top_value):
    def one(axis_at, shards_of):
        draws = jax.random.uniform(jax.random.fold_in(jax.random.fold_in(own_key, 6), axis_at), (shards_of,), jnp.float32, smallest / len(pieces), top_value / len(pieces))
        return jnp.repeat(jnp.exp(draws), shape[axis_at] // shards_of).reshape((-1,) + (1,) * (len(shape) - axis_at - 1))

    factor_of = one(*pieces[0])
    for cut in pieces[1:]:
        factor_of = factor_of * one(*cut)
    return factor_of


def normal_values(rng, dims, deviation, limit, shards=(), kind=jnp.bfloat16):
    result = deviation * jax.random.normal(rng, dims, jnp.float32)
    if shards:
        result = result * block_scale(rng, dims, shards, -0.22, 0.18)
    return jnp.clip(result, -limit, limit).astype(kind)


def setup_inputs(seed: int = 0) -> dict:
    seeds = jax.random.split(jax.random.key(seed), 5)
    return {
        "tokens": normal_values(seeds[0], (TOKENS, D), 1.0, 6.0, ((0, 8), (1, 4))),
        "w_up": normal_values(seeds[1], (D, F), D ** -0.5, 0.09375, ((0, 4), (1, 2))),
        "w_down": normal_values(seeds[2], (D, F), F ** -0.5, 0.046875, ((0, 4), (1, 2))),
        "cotangent": normal_values(seeds[3], (TOKENS, D), 1.0, 6.0, ((0, 8), (1, 4))),
    }


gelu_coef = 0.7978845608
cubic_coef = 0.044715


def rounded(matrix):
    return lax.optimization_barrier(matrix.astype(jnp.bfloat16)).astype(jnp.float32)


def gelu_pair(hidden):
    tangent = jnp.tanh(gelu_coef * (hidden + cubic_coef * hidden * hidden * hidden))
    activated = 0.5 * hidden * (1.0 + tangent)
    derivative = 0.5 * (1.0 + tangent) + 0.5 * hidden * (1.0 - tangent * tangent) * gelu_coef * (1.0 + 3.0 * cubic_coef * hidden * hidden)
    return activated, derivative


def reference(tokens, w_up, w_down, cotangent):
    width_block = D // N_ROW
    hidden = jnp.zeros((tokens.shape[0], F), jnp.float32)
    back = jnp.zeros((tokens.shape[0], F), jnp.float32)
    for index_row in range(N_ROW):
        first = index_row * width_block
        hidden = hidden + rounded(jnp.dot(tokens[:, first:first + width_block], w_up[first:first + width_block], preferred_element_type=jnp.float32))
        back = back + rounded(jnp.dot(cotangent[:, first:first + width_block], w_down[first:first + width_block], preferred_element_type=jnp.float32))
    activated, derivative = gelu_pair(hidden)
    activated = activated.astype(jnp.bfloat16)
    output = jnp.dot(activated, w_down.T, preferred_element_type=jnp.float32).astype(jnp.bfloat16)
    hidden_grad = (back * derivative).astype(jnp.bfloat16)
    input_grad = jnp.dot(hidden_grad, w_up.T, preferred_element_type=jnp.float32).astype(jnp.bfloat16)
    grad_scale = float(TOKENS) ** -0.5
    up_grad = grad_scale * jnp.dot(tokens.T, hidden_grad, preferred_element_type=jnp.float32)
    down_grad = grad_scale * jnp.dot(cotangent.T, activated, preferred_element_type=jnp.float32)
    return output, input_grad, up_grad, down_grad
```

```python
import jax
import jax.numpy as jnp
from jax import lax
from jax.experimental import pallas as pl
from jax.experimental.pallas import tpu as pltpu
from jax.sharding import PartitionSpec as P

gelu_coef = 0.7978845608
cubic_coef = 0.044715
bf16 = jnp.bfloat16
f32 = jnp.float32


def gelu_pair(hidden):
    tangent = jnp.tanh(gelu_coef * (hidden + cubic_coef * hidden * hidden * hidden))
    activated = 0.5 * hidden * (1.0 + tangent)
    derivative = 0.5 * (1.0 + tangent) + 0.5 * hidden * (1.0 - tangent * tangent) * gelu_coef * (
        1.0 + 3.0 * cubic_coef * hidden * hidden
    )
    return (activated, derivative)


def times(left, right):
    return jnp.dot(left, right, preferred_element_type=f32)


def times_transposed(left, right):
    return lax.dot_general(left, right, (((1,), (1,)), ((), ())), preferred_element_type=f32)


def over_tokens(left, right):
    return lax.dot_general(left, right, (((0,), (0,)), ((), ())), preferred_element_type=f32)


def tie(*values):
    return lax.optimization_barrier(values)


def total_of(end, term, first, middle, third):
    inside = first[...].astype(f32) + middle[...].astype(f32)
    return term[...].astype(f32) + jnp.where(end, third[...].astype(f32), inside)


def in_hbm(value):
    return pltpu.with_memory_space_constraint(value, pltpu.HBM)


def in_vmem(value):
    return pltpu.with_memory_space_constraint(value, pltpu.VMEM)


def put_blocks(places, pairs, sems):
    copies = []
    for k, (tile, whole) in enumerate(pairs):
        rows = tile.shape[0]
        start = pl.multiple_of(places[0] * rows, rows)
        copies.append(pltpu.make_async_copy(tile, whole.at[pl.ds(start, rows)], sems.at[k]))
    for copy in copies:
        copy.start()
    for copy in copies:
        copy.wait()


def forward_kernel(places, term, first, middle, third, *refs):
    act, der, act_tile, der_tile, sems = refs[-5:]
    hidden = total_of(places[1] == 1, term, first, middle, third)
    activated, derivative = gelu_pair(hidden)
    act_tile[...] = activated.astype(bf16)
    der_tile[...] = derivative.astype(bf16)
    put_blocks(places, [(act_tile, act), (der_tile, der)], sems)


def backward_kernel(places, term, first, middle, third, der, *refs):
    grad, block, sems = refs[-3:]
    back = total_of(places[1] == 1, term, first, middle, third)
    block[...] = (back * der[...].astype(f32)).astype(bf16)
    put_blocks(places, [(block, grad)], sems)


def finish_call(kernel, places, parts, reads, held, whole_shape, n_whole, flat):
    rows, width = parts[0].shape
    at_block = pl.BlockSpec((rows, width), lambda j, p: (p[0], 0))
    plain = pl.BlockSpec((rows, width), lambda j, p: (0, 0))
    in_specs = [plain] * len(parts) + [at_block] * len(reads)
    in_specs += [pl.BlockSpec(memory_space=pltpu.HBM)] * len(held)
    tiles = [] if flat else [pltpu.VMEM((rows, width), bf16)] * n_whole
    out_shape = [jax.ShapeDtypeStruct(whole_shape, bf16)] * n_whole
    out_shape += [jax.ShapeDtypeStruct((rows, width), bf16)] * flat
    first_held = 1 + len(parts) + len(reads)
    return pl.pallas_call(
        kernel,
        grid_spec=pltpu.PrefetchScalarGridSpec(
            num_scalar_prefetch=1,
            grid=(1,),
            in_specs=in_specs,
            out_specs=[pl.BlockSpec(memory_space=pltpu.HBM)] * n_whole + [plain] * flat,
            scratch_shapes=tiles + [pltpu.SemaphoreType.DMA((n_whole,))],
        ),
        out_shape=out_shape,
        input_output_aliases={first_held + k: k for k in range(len(held))},
        compiler_params=pltpu.CompilerParams(vmem_limit_bytes=16 * 2**20),
        cost_estimate=pl.CostEstimate(
            flops=40 * rows * width, bytes_accessed=14 * rows * width, transcendentals=rows * width
        ),
    )(places, *[in_vmem(v) for v in parts], *[in_hbm(v) for v in reads + held])


def slice_kernel(place, x, w, term, piece):
    value = w[...]
    piece[...] = value
    product = lax.dot_general(value, x[...], (((0,), (1,)), ((), ())), preferred_element_type=f32)
    term[...] = product.T.astype(bf16)


def column_tile(width):
    return next(t for t in (1024, 512, 256, 128, width) if width % t == 0)


def slice_call(place, x, w, width):
    rows, depth = x.shape
    tile = column_tile(width)
    steps = width // tile
    return pl.pallas_call(
        slice_kernel,
        grid_spec=pltpu.PrefetchScalarGridSpec(
            num_scalar_prefetch=1,
            grid=(steps,),
            in_specs=[
                pl.BlockSpec((rows, depth), lambda j, p: (0, 0)),
                pl.BlockSpec((depth, tile), lambda j, p: (0, p[0] * steps + j)),
            ],
            out_specs=[
                pl.BlockSpec((rows, tile), lambda j, p: (0, j)),
                pl.BlockSpec((depth, tile), lambda j, p: (0, j)),
            ],
        ),
        out_shape=[
            jax.ShapeDtypeStruct((rows, width), bf16),
            jax.ShapeDtypeStruct((depth, width), bf16),
        ],
        compiler_params=pltpu.CompilerParams(vmem_limit_bytes=16 * 2**20),
        cost_estimate=pl.CostEstimate(
            flops=2 * rows * depth * width, bytes_accessed=4 * depth * width, transcendentals=0
        ),
    )(place, x, in_hbm(w))


def body(tokens, w_up, w_down, cotangent):
    n_dp, n_col, n_row = (lax.axis_size(a) for a in ("dp", "col", "row"))
    n = n_dp * n_col
    rows = tokens.shape[0]
    grad_scale = float(rows * n) ** (-0.5)
    piece = w_up.shape[1] // n_dp
    me = lax.axis_index("dp") * n_col + lax.axis_index("col")
    at = lax.axis_index("row")
    end = (at == 0) | (at == n_row - 1)
    plane = ("dp", "col")
    place = jnp.stack([lax.axis_index("dp")]).astype(jnp.int32)

    def peer(i, s):
        return i ^ s if n & (n - 1) == 0 else (i + s) % n

    def to_peer(value, s):
        return lax.ppermute(value, plane, [(i, peer(i, s)) for i in range(n)])

    outer = [(0, 1), (1, 0), (3, 2), (2, 3)]
    inner = [(1, 2), (2, 1)]

    order = [("h", 0), ("h", 1), ("b", 1)]
    order += [("h", s) for s in range(2, n)] + [("b", s) for s in range(2, n)] + [("b", 0)]
    total = len(order)
    step_of = {u: i for i, u in enumerate(order)}
    forward_done = step_of["h", n - 1] + 3

    beside = to_peer(jnp.stack([tokens, cotangent]), 1)
    first_term, own_up = slice_call(place, tokens, w_up, piece)
    tokens_all = lax.all_gather(tokens, plane, axis=0, tiled=True)
    grads_all = lax.all_gather(cotangent, plane, axis=0, tiled=True)

    term, merged, first, middle, early = {0: first_term}, {}, {}, {}, {}
    whole = {}
    sent, landed = {}, {}
    results = {}
    act = der = grad = e = None
    for t in range(total + 3):
        e_in = m_in = None
        if t < 2:
            e_in = term[t]
        elif t < total + 2:
            e_in = (middle[t - 2].astype(f32) + merged[t].astype(f32)).astype(bf16)
        if 1 <= t <= total:
            m_in = (first[t - 1].astype(f32) + term[t - 1].astype(f32)).astype(bf16)
        names = ["e_in", "m_in", "third"]
        heads = dict(zip(names, (e_in, m_in, e)))
        heads = {k: v for k, v in heads.items() if v is not None}
        gate = {k: v for k, v in whole.items()}
        gate["own_up"] = own_up
        if act is not None:
            gate["act"] = act
        if t >= 1:
            gate["tokens"] = tokens
            gate["cotangent"] = cotangent
        got = dict(zip(list(heads) + list(gate), tie(*heads.values(), *gate.values())))
        own_up = got["own_up"]
        act = got.get("act", act)
        tokens, cotangent = got.get("tokens", tokens), got.get("cotangent", cotangent)
        for k in whole:
            whole[k] = got[k]
        e = lax.ppermute(got["e_in"], "row", outer) if e_in is not None else None
        m = lax.ppermute(got["m_in"], "row", inner) if m_in is not None else None
        third = got.get("third")
        fresh = {}
        if t == 0:
            term[1] = times(beside[0], own_up).astype(bf16)
            fresh["term", 1] = term[1]
        if t == 1:
            both, own_down = slice_call(place, jnp.concatenate([cotangent, beside[1]]), w_down, piece)
            whole["own_down"] = fresh["whole", "own_down"] = own_down
            term[2], own_last = both[rows:], both[:rows]
            fresh["term", 2] = term[2]
        if t == 2:
            whole["h"] = fresh["whole", "h"] = times(tokens_all, own_up).astype(bf16)
        if t == 5:
            whole["b"] = fresh["whole", "b"] = times(grads_all, whole["own_down"]).astype(bf16)
        if t == 3:
            whole["tokens_t"] = fresh["whole", "tokens_t"] = tokens_all.T
        if t == 7:
            whole["grads_t"] = fresh["whole", "grads_t"] = grads_all.T
        u = t - 3
        if u >= 0:
            kind, s = order[u]
            places = jnp.stack([peer(me, s), end.astype(jnp.int32)]).astype(jnp.int32)
            parts = [term[u], first[u], middle[u], third]
            shape = (n * rows, piece)
            if kind == "h":
                held = [] if act is None else [act, der]
                act, der = finish_call(forward_kernel, places, parts, [], held, shape, 2, 0)
            else:
                held = [] if grad is None else [grad]
                grad, block = finish_call(backward_kernel, places, parts, [der], held, shape, 1, 1)
                part = times_transposed(own_up, block).T
                if s == 0:
                    part_own = part
                else:
                    sent[s] = part.astype(bf16)
                    fresh["sent", s] = sent[s]
        if t == forward_done:
            fresh["result", "out"] = times_transposed(act, whole["own_down"]).astype(bf16)
        if t == forward_done + 2:
            fresh["result", "down"] = grad_scale * times(whole["grads_t"], act)
        if t + 1 < total and t + 1 not in term:
            kind, s = order[t + 1]
            if (kind, s) == ("b", 0):
                term[t + 1] = own_last
            else:
                term[t + 1] = lax.dynamic_slice_in_dim(whole[kind], peer(me, s) * rows, rows, axis=0)
        if 2 <= t + 1 < total + 2:
            late = term[t - 1]
            merged[t + 1] = jnp.where(end, term[t + 1], late) if t + 1 < total else late
        if t + 1 in term:
            fresh["term", t + 1] = term[t + 1]
        if t + 1 in merged:
            fresh["merged", t + 1] = merged[t + 1]
        for s in [s for s in landed if landed[s][0] == t]:
            fresh["landed", s] = landed[s][1]
        for k, v in (("act", act), ("der", der), ("grad", grad)):
            if v is not None:
                fresh["state", k] = v
        if e is not None:
            fresh["e", t] = e
        if m is not None:
            fresh["m", t] = m
        got = dict(zip(fresh, tie(*fresh.values())))
        for (store, k), v in got.items():
            if store == "term":
                term[k] = v
            elif store == "merged":
                merged[k] = v
            elif store == "whole":
                whole[k] = v
            elif store == "result":
                results[k] = v
            elif store == "landed":
                landed[k] = (-1, v)
            elif store == "sent":
                landed[k] = (t + 2, to_peer(v, k))
        e = got.get(("e", t))
        if e is not None:
            first[t] = e
        if m is not None:
            middle[t - 1] = got["m", t]
        act, der, grad = (got.get(("state", k), v) for k, v in (("act", act), ("der", der), ("grad", grad)))
        if ("result", "out") in got:
            landed["out"] = (t + 5, lax.psum_scatter(results["out"], plane, scatter_dimension=0, tiled=True))
    input_grad = part_own
    for s in range(1, n):
        input_grad = input_grad + landed[s][1].astype(f32)
    up_grad = grad_scale * times(whole["tokens_t"], grad)
    return (landed["out"][1], input_grad.astype(bf16), up_grad, results["down"])


def solution(mesh):
    placed = (P(("dp", "col"), "row"), P("row", "col"), P("row", "col"), P(("dp", "col"), "row"))
    return jax.shard_map(
        body,
        mesh=mesh,
        in_specs=placed,
        out_specs=(
            P(("dp", "col"), "row"),
            P(("dp", "col"), "row"),
            P("row", ("col", "dp")),
            P("row", ("col", "dp")),
        ),
        check_vma=False,
    )
```

```python
import functools

import jax
import jax.numpy as jnp
from jax import lax
from jax.experimental import pallas as pl
from jax.experimental.pallas import tpu as pltpu
from jax.sharding import PartitionSpec as P

gelu_coef = 0.7978845608
cubic_coef = 0.044715
bf16 = jnp.bfloat16
f32 = jnp.float32


def gelu_pair(hidden):
    tangent = jnp.tanh(gelu_coef * (hidden + cubic_coef * hidden * hidden * hidden))
    activated = 0.5 * hidden * (1.0 + tangent)
    derivative = 0.5 * (1.0 + tangent) + 0.5 * hidden * (1.0 - tangent * tangent) * gelu_coef * (
        1.0 + 3.0 * cubic_coef * hidden * hidden
    )
    return (activated, derivative)


def times(left, right):
    return jnp.dot(left, right, preferred_element_type=f32)


def times_transposed(left, right):
    return lax.dot_general(left, right, (((1,), (1,)), ((), ())), preferred_element_type=f32)


brief = pl.CostEstimate(flops=1, bytes_accessed=1, transcendentals=0)


def tie(*values):
    return lax.optimization_barrier(values)


def total_of(end, term, first, middle, third):
    inside = first[...].astype(f32) + middle[...].astype(f32)
    return term[...].astype(f32) + jnp.where(end, third[...].astype(f32), inside)


def in_hbm(value):
    return pltpu.with_memory_space_constraint(value, pltpu.HBM)


def in_vmem(value):
    return pltpu.with_memory_space_constraint(value, pltpu.VMEM)


def put_blocks(index, pairs, sems):
    copies = []
    for k, (tile, whole) in enumerate(pairs):
        rows = tile.shape[0]
        start = pl.multiple_of(index * rows, rows)
        copies.append(pltpu.make_async_copy(tile, whole.at[pl.ds(start, rows)], sems.at[k]))
    for copy in copies:
        copy.start()
    for copy in copies:
        copy.wait()


def forward_kernel(at, places, term, first, middle, third, *refs):
    act, der, act_tile, der_tile, sems = refs[-5:]
    hidden = total_of(places[0] == 1, term, first, middle, third)
    activated, derivative = gelu_pair(hidden)
    act_tile[...] = activated.astype(bf16)
    der_tile[...] = derivative.astype(bf16)
    put_blocks(places[at], [(act_tile, act), (der_tile, der)], sems)


def backward_kernel(at, places, term, first, middle, third, der, w, *refs):
    grad, part, block, sems = refs[-4:]
    rows = block.shape[0]
    start = pl.multiple_of(places[at] * rows, rows)
    save = pltpu.make_async_copy(block, grad.at[pl.ds(start, rows)], sems.at[0])
    step = pl.program_id(0)

    @pl.when(step == 0)
    def _():
        back = total_of(places[0] == 1, term, first, middle, third)
        block[...] = (back * der[...].astype(f32)).astype(bf16)
        save.start()

    product = lax.dot_general(w[...], block[...], (((1,), (1,)), ((), ())), preferred_element_type=f32)
    part[...] = product.T.astype(part.dtype)

    @pl.when(step == pl.num_programs(0) - 1)
    def _():
        save.wait()


def forward_call(places, at, parts, held, shape):
    rows, width = parts[0].shape
    plain = pl.BlockSpec((rows, width), lambda j, p: (0, 0))
    whole = pl.BlockSpec(memory_space=pltpu.HBM)
    return pl.pallas_call(
        functools.partial(forward_kernel, at),
        grid_spec=pltpu.PrefetchScalarGridSpec(
            num_scalar_prefetch=1,
            grid=(1,),
            in_specs=[plain] * 4 + [whole] * len(held),
            out_specs=[whole] * 2,
            scratch_shapes=[pltpu.VMEM((rows, width), bf16)] * 2 + [pltpu.SemaphoreType.DMA((2,))],
        ),
        out_shape=[pltpu.HBM(shape, bf16)] * 2,
        input_output_aliases={5 + k: k for k in range(len(held))},
        compiler_params=pltpu.CompilerParams(vmem_limit_bytes=16 * 2**20),
        cost_estimate=brief,
    )(places, *[in_vmem(v) for v in parts], *[in_hbm(v) for v in held])


def backward_call(places, at, parts, der, w, grad, pack, side, kind):
    rows, width = parts[0].shape
    depth = w.shape[0]
    held = [(k, v) for k, v in ((0, grad), (1, pack)) if v is not None]
    tile = column_tile(depth) // 2
    plain = pl.BlockSpec((rows, width), lambda j, p: (0, 0))
    whole = pl.BlockSpec(memory_space=pltpu.HBM)
    return pl.pallas_call(
        functools.partial(backward_kernel, at),
        grid_spec=pltpu.PrefetchScalarGridSpec(
            num_scalar_prefetch=1,
            grid=(depth // tile,),
            in_specs=[plain] * 4
            + [
                pl.BlockSpec((rows, width), lambda j, p: (p[at], 0)),
                pl.BlockSpec((tile, width), lambda j, p: (j, 0)),
            ]
            + [whole] * len(held),
            out_specs=[whole, pl.BlockSpec((rows, tile), lambda j, p: (side if pack is not None else 0, j))],
            scratch_shapes=[pltpu.VMEM((rows, width), bf16), pltpu.SemaphoreType.DMA((1,))],
        ),
        out_shape=[
            pltpu.HBM(der.shape, bf16),
            jax.ShapeDtypeStruct((2 * rows if side is not None else rows, depth), kind),
        ],
        input_output_aliases={7 + i: k for i, (k, _) in enumerate(held)},
        compiler_params=pltpu.CompilerParams(vmem_limit_bytes=20 * 2**20),
        cost_estimate=brief,
    )(places, *[in_vmem(v) for v in parts], in_hbm(der), in_hbm(w), *[in_hbm(v) for _, v in held])


def column_tile(width):
    return next(t for t in (1024, 512, 256, 128, width) if width % t == 0)


def slice_kernel(place, x, w, term, piece):
    value = w[...]
    piece[...] = value
    product = lax.dot_general(value, x[...], (((0,), (1,)), ((), ())), preferred_element_type=f32)
    term[...] = product.T.astype(bf16)


def slice_call(place, x, w, width):
    rows, depth = x.shape
    tile = column_tile(width)
    steps = width // tile
    return pl.pallas_call(
        slice_kernel,
        grid_spec=pltpu.PrefetchScalarGridSpec(
            num_scalar_prefetch=1,
            grid=(steps,),
            in_specs=[
                pl.BlockSpec((rows, depth), lambda j, p: (0, 0)),
                pl.BlockSpec((depth, tile), lambda j, p: (0, p[2] * steps + j)),
            ],
            out_specs=[
                pl.BlockSpec((rows, tile), lambda j, p: (0, j)),
                pl.BlockSpec((depth, tile), lambda j, p: (0, j)),
            ],
        ),
        out_shape=[
            jax.ShapeDtypeStruct((rows, width), bf16),
            pltpu.HBM((depth, width), bf16),
        ],
        compiler_params=pltpu.CompilerParams(vmem_limit_bytes=16 * 2**20),
        cost_estimate=brief,
    )(place, x, in_hbm(w))


def pair_kernel(places, x_a, x_b, w, a, b):
    x = jnp.concatenate([x_a[...], x_b[...]], axis=0)
    product = lax.dot_general(w[...], x, (((0,), (1,)), ((), ())), preferred_element_type=f32)
    both = product.T.astype(bf16)
    rows = x_a.shape[0]
    a[...] = both[:rows]
    b[...] = both[rows:]


def pair_call(places, at, side, x, w, rows):
    depth, width = w.shape
    tile = column_tile(width)
    flat = pl.BlockSpec((rows, tile), lambda j, p: (0, j))
    return pl.pallas_call(
        pair_kernel,
        grid_spec=pltpu.PrefetchScalarGridSpec(
            num_scalar_prefetch=1,
            grid=(width // tile,),
            in_specs=[
                pl.BlockSpec((rows, depth), lambda j, p: (2 * p[at] + side, 0)),
                pl.BlockSpec((rows, depth), lambda j, p: (2 * p[at + 1] + side, 0)),
                pl.BlockSpec((depth, tile), lambda j, p: (0, j)),
            ],
            out_specs=[flat] * 2,
        ),
        out_shape=[pltpu.VMEM((rows, width), bf16)] * 2,
        compiler_params=pltpu.CompilerParams(vmem_limit_bytes=20 * 2**20),
        cost_estimate=brief,
    )(places, in_hbm(x), in_hbm(x), in_hbm(w))


def unset(shapes, kind=bf16):
    return pl.pallas_call(
        lambda *refs: None,
        out_specs=[pl.BlockSpec(memory_space=pltpu.HBM)] * len(shapes),
        out_shape=[pltpu.HBM(shape, kind) for shape in shapes],
    )()


def body(tokens, w_up, w_down, cotangent):
    n_dp, n_col, n_row = (lax.axis_size(a) for a in ("dp", "col", "row"))
    n = n_dp * n_col
    rows, depth = tokens.shape
    grad_scale = float(rows * n) ** (-0.5)
    piece = w_up.shape[1] // n_dp
    dp, col, at = (lax.axis_index(a) for a in ("dp", "col", "row"))
    me = dp * n_col + col
    end = (at == 0) | (at == n_row - 1)
    def block(k, j):
        return (dp ^ k) * n_col + (col ^ j)

    def to_chip(value, k):
        return lax.ppermute(value, "dp", [(i, i ^ k) for i in range(n_dp)])

    def to_beside(value):
        return lax.ppermute(value, "col", [(0, 1), (1, 0)])

    outer = [(0, 1), (1, 0), (3, 2), (2, 3)]
    inner = [(1, 2), (2, 1)]

    chips = list(range(n_dp - 1, 0, -1))
    order = [("h", 0, 0), ("h", 0, 1), ("b", 0, 1)]
    order += [(kind, k, j) for kind in "hb" for k in chips for j in (0, 1)] + [("b", 0, 0)]
    total = len(order)
    forward_done = order.index(("h", chips[-1], 1)) + 3
    last = total + 2
    named = 3
    places = [end, me, dp] + [block(k, j) for _, k, j in order]
    places = jnp.stack([x.astype(jnp.int32) for x in places])
    places, end, col, tokens, cotangent = tie(places, end, col, tokens, cotangent)
    ahead = order.index(("b", chips[0], 0))
    pairs = {v - 1: v for v in range(3, ahead, 2)}
    for v in range(ahead, total - 1, 2):
        pairs[next(t for t in range(ahead - 2, total) if t not in pairs)] = v

    beside_t = to_beside(tokens)
    first_term, own_up = slice_call(places, tokens, w_up, piece)
    both_all = lax.all_gather(jnp.concatenate([tokens, cotangent]), ("dp", "col"), axis=0, tiled=True)
    beside_g = to_beside(cotangent)
    g_pair = jnp.concatenate([cotangent, beside_g])
    g_terms = lax.cond(
        col == 1,
        lambda p, x, w, y, v: (*slice_call(p, x, w, piece), times(y, v).astype(bf16)),
        lambda p, x, w, y, v: tuple(unset([(n_col * rows, piece), (depth, piece), (rows, piece)])),
        places,
        g_pair,
        w_down,
        beside_t,
        own_up,
    )

    term, first, middle = {0: first_term}, {}, {}
    whole, landed, own = {}, {}, {}
    state = {}
    e = None
    for t in range(total + 3):
        heads = {}
        if t < 2:
            heads["e_in"] = term[t]
        elif t < total + 2:
            heads["e_in"] = (middle[t - 2].astype(f32) + term[t - 2].astype(f32)).astype(bf16)
            if t < total:
                heads["e_in"] = jnp.where(end, term[t], heads["e_in"])
        if 1 <= t <= total:
            heads["m_in"] = (first[t - 1].astype(f32) + term[t - 1].astype(f32)).astype(bf16)
        if e is not None:
            heads["third"] = e
        if t == 0:
            heads.update({("g_terms", i): x for i, x in enumerate(g_terms)})
        if t == 1:
            heads["g_pair"] = g_pair
        if t >= 1:
            heads["own_up"] = own_up
            heads["tokens"] = tokens
            heads["cotangent"] = cotangent
            heads.update({("state", k): v for k, v in state.items()})
            heads.update({("whole", k): v for k, v in whole.items()})
        if t == last:
            heads.update({("landed", k): v[1] for k, v in landed.items()})
        heads = dict(zip(heads, tie(*heads.values())))
        if t == last:
            landed = {k: (-1, heads["landed", k]) for k in landed}
        own_up = heads.get("own_up", own_up)
        tokens, cotangent = heads.get("tokens", tokens), heads.get("cotangent", cotangent)
        state = {k: heads["state", k] for k in state}
        whole = {k: heads["whole", k] for k in whole}
        if t == 0:
            g_terms = [heads["g_terms", i] for i in range(3)]
        third = heads.get("third")
        fresh = {}
        if "e_in" in heads:
            fresh["e"] = lax.ppermute(heads["e_in"], "row", outer)
        if "m_in" in heads:
            fresh["m"] = lax.ppermute(heads["m_in"], "row", inner)
        if t == 0:
            term[1] = lax.cond(
                col == 1,
                lambda y, v, done: done,
                lambda y, v, done: times(y, v).astype(bf16),
                beside_t,
                own_up,
                g_terms[2],
            )
            fresh["term", 1] = term[1]
        if t == 1:
            both, own_down = lax.cond(
                col == 1,
                lambda p, x, w, done: tuple(done),
                lambda p, x, w, done: tuple(slice_call(p, x, w, piece)),
                places,
                heads["g_pair"],
                w_down,
                g_terms[:2],
            )
            term[2], own_last = both[rows:], both[:rows]
            whole["down"] = own_down
            fresh["whole", "down"] = own_down
            fresh["term", 2] = term[2]
            fresh["term", total - 1] = own_last
        if t in (4, 10):
            parted = whole["both"].reshape(n, 2, rows, depth)
            name, side = ("tokens_t", 0) if t == 4 else ("grads_t", 1)
            fresh["whole", name] = parted[:, side].reshape(n * rows, depth).T
        u = t - 3
        if u >= 0:
            kind, k, j = order[u]
            parts = [term[u], first[u], middle[u], third]
            if kind == "h":
                held = [state["act"], state["der"]] if "act" in state else []
                state["act"], state["der"] = forward_call(places, named + u, parts, held, (n * rows, piece))
            else:
                single = k in (0, chips[-1])
                state["grad"], part = backward_call(
                    places,
                    named + u,
                    parts,
                    state["der"],
                    own_up,
                    state.get("grad"),
                    whole.pop("pack", None),
                    None if single else j,
                    f32 if k == 0 else bf16,
                )
                if k == 0:
                    fresh["own", j] = part
                elif single and j == 1:
                    landed[k, j] = (last, to_chip(part, k))
                elif single:
                    fresh["send", (k, j)] = part
                elif j == 0:
                    fresh["whole", "pack"] = part
                else:
                    fresh["send", (k, None)] = part
        n_half = n * rows // 2
        if t == forward_done:
            fresh["whole", "out"] = times_transposed(state["act"][:n_half], whole["down"]).astype(bf16)
        if t == forward_done + 1:
            rest = times_transposed(state["act"][n_half:], whole["down"]).astype(bf16)
            fresh["out", 0] = jnp.concatenate([whole.pop("out"), rest])
        if t in (forward_done + 2, forward_done + 4):
            at_row = 0 if t == forward_done + 2 else depth // 2
            part = grad_scale * times(whole["grads_t"][at_row : at_row + depth // 2], state["act"])
            down_grad = whole.get("down_grad")
            if down_grad is None:
                (down_grad,) = unset([(depth, piece)], f32)
            fresh["whole", "down_grad"] = lax.dynamic_update_slice(down_grad, part, (at_row, 0))
        if t in pairs:
            v = pairs[t]
            kind, k, j = order[v]
            side, w = (0, own_up) if kind == "h" else (1, whole["down"])
            both = whole.get("both", both_all)
            term[v], term[v + 1] = pair_call(places, named + v, side, both, w, rows)
            if "both" not in whole:
                fresh["whole", "both"] = both
            fresh["term", v], fresh["term", v + 1] = term[v], term[v + 1]
        for key in [key for key in landed if landed[key][0] == t]:
            fresh["landed", key] = landed[key][1]
        fresh.update({("state", k): x for k, x in state.items()})
        fresh = dict(zip(fresh, tie(*fresh.values())))
        e = fresh.get("e")
        if e is not None:
            first[t] = e
        if "m" in fresh:
            middle[t - 1] = fresh["m"]
        for key, x in fresh.items():
            if not isinstance(key, tuple):
                continue
            store, k = key
            if store == "landed":
                landed[k] = (-1, x)
            elif store == "send":
                landed[k] = (min(t + 3, last - 1), to_chip(x, k[0]))
            elif store == "out":
                output = lax.psum_scatter(x, ("dp", "col"), scatter_dimension=0, tiled=True)
            else:
                {"term": term, "whole": whole, "state": state, "own": own}[store][k] = x
    sums = [own[0], own[1]]
    for k, side in landed:
        part = landed[k, side][1].astype(f32)
        for j in (0, 1):
            if side is None:
                sums[j] = sums[j] + part[j * rows : (j + 1) * rows]
            elif side == j:
                sums[j] = sums[j] + part
    input_grad = sums[0] + to_beside(sums[1].astype(bf16)).astype(f32)
    up_grad = grad_scale * times(whole["tokens_t"], state["grad"])
    return (output, input_grad.astype(bf16), up_grad, whole["down_grad"])


def solution(mesh):
    placed = (P(("dp", "col"), "row"), P("row", "col"), P("row", "col"), P(("dp", "col"), "row"))
    return jax.shard_map(
        body,
        mesh=mesh,
        in_specs=placed,
        out_specs=(
            P(("dp", "col"), "row"),
            P(("dp", "col"), "row"),
            P("row", ("col", "dp")),
            P("row", ("col", "dp")),
        ),
        check_vma=False,
    )
```

```python
import functools

import jax
import jax.numpy as jnp
from jax import lax
from jax.experimental import pallas as pl
from jax.experimental.pallas import tpu as pltpu
from jax.sharding import PartitionSpec as P

gelu_coef = 0.7978845608
cubic_coef = 0.044715
bf16 = jnp.bfloat16
f32 = jnp.float32


def gelu_pair(hidden):
    tangent = jnp.tanh(gelu_coef * (hidden + cubic_coef * hidden * hidden * hidden))
    activated = 0.5 * hidden * (1.0 + tangent)
    derivative = 0.5 * (1.0 + tangent) + 0.5 * hidden * (1.0 - tangent * tangent) * gelu_coef * (
        1.0 + 3.0 * cubic_coef * hidden * hidden
    )
    return (activated, derivative)


def times(left, right):
    return jnp.dot(left, right, preferred_element_type=f32)


def times_transposed(left, right):
    return lax.dot_general(left, right, (((1,), (1,)), ((), ())), preferred_element_type=f32)


brief = pl.CostEstimate(flops=1, bytes_accessed=1, transcendentals=0)


def tie(*values):
    return lax.optimization_barrier(values)


def total_of(end, term, first, middle, third):
    inside = first[...].astype(f32) + middle[...].astype(f32)
    return term[...].astype(f32) + jnp.where(end, third[...].astype(f32), inside)


def in_hbm(value):
    return pltpu.with_memory_space_constraint(value, pltpu.HBM)


def in_vmem(value):
    return pltpu.with_memory_space_constraint(value, pltpu.VMEM)


def put_blocks(index, pairs, sems):
    copies = []
    for k, (tile, whole) in enumerate(pairs):
        rows = tile.shape[0]
        start = pl.multiple_of(index * rows, rows)
        copies.append(pltpu.make_async_copy(tile, whole.at[pl.ds(start, rows)], sems.at[k]))
    for copy in copies:
        copy.start()
    for copy in copies:
        copy.wait()


def forward_kernel(at, places, term, first, middle, third, *refs):
    act, der, act_tile, der_tile, sems = refs[-5:]
    hidden = total_of(places[0] == 1, term, first, middle, third)
    activated, derivative = gelu_pair(hidden)
    act_tile[...] = activated.astype(bf16)
    der_tile[...] = derivative.astype(bf16)
    put_blocks(places[at], [(act_tile, act), (der_tile, der)], sems)


def backward_kernel(at, places, term, first, middle, third, der, w, *refs):
    grad, part, block, sems = refs[-4:]
    rows = block.shape[0]
    start = pl.multiple_of(places[at] * rows, rows)
    save = pltpu.make_async_copy(block, grad.at[pl.ds(start, rows)], sems.at[0])
    step = pl.program_id(0)

    @pl.when(step == 0)
    def _():
        back = total_of(places[0] == 1, term, first, middle, third)
        block[...] = (back * der[...].astype(f32)).astype(bf16)
        save.start()

    product = lax.dot_general(w[...], block[...], (((1,), (1,)), ((), ())), preferred_element_type=f32)
    part[...] = product.T.astype(part.dtype)

    @pl.when(step == pl.num_programs(0) - 1)
    def _():
        save.wait()


def forward_call(places, at, parts, held, shape):
    rows, width = parts[0].shape
    plain = pl.BlockSpec((rows, width), lambda j, p: (0, 0))
    whole = pl.BlockSpec(memory_space=pltpu.HBM)
    return pl.pallas_call(
        functools.partial(forward_kernel, at),
        grid_spec=pltpu.PrefetchScalarGridSpec(
            num_scalar_prefetch=1,
            grid=(1,),
            in_specs=[plain] * 4 + [whole] * len(held),
            out_specs=[whole] * 2,
            scratch_shapes=[pltpu.VMEM((rows, width), bf16)] * 2 + [pltpu.SemaphoreType.DMA((2,))],
        ),
        out_shape=[pltpu.HBM(shape, bf16)] * 2,
        input_output_aliases={5 + k: k for k in range(len(held))},
        compiler_params=pltpu.CompilerParams(vmem_limit_bytes=16 * 2**20),
        cost_estimate=brief,
    )(places, *[in_vmem(v) for v in parts], *[in_hbm(v) for v in held])


def backward_call(places, at, parts, der, w, grad, pack, side, kind):
    rows, width = parts[0].shape
    depth = w.shape[0]
    held = [(k, v) for k, v in ((0, grad), (1, pack)) if v is not None]
    tile = column_tile(depth) // 2
    plain = pl.BlockSpec((rows, width), lambda j, p: (0, 0))
    whole = pl.BlockSpec(memory_space=pltpu.HBM)
    return pl.pallas_call(
        functools.partial(backward_kernel, at),
        grid_spec=pltpu.PrefetchScalarGridSpec(
            num_scalar_prefetch=1,
            grid=(depth // tile,),
            in_specs=[plain] * 4
            + [
                pl.BlockSpec((rows, width), lambda j, p: (p[at], 0)),
                pl.BlockSpec((tile, width), lambda j, p: (j, 0)),
            ]
            + [whole] * len(held),
            out_specs=[whole, pl.BlockSpec((rows, tile), lambda j, p: (side if pack is not None else 0, j))],
            scratch_shapes=[pltpu.VMEM((rows, width), bf16), pltpu.SemaphoreType.DMA((1,))],
        ),
        out_shape=[
            pltpu.HBM(der.shape, bf16),
            jax.ShapeDtypeStruct((2 * rows if side is not None else rows, depth), kind),
        ],
        input_output_aliases={7 + i: k for i, (k, _) in enumerate(held)},
        compiler_params=pltpu.CompilerParams(vmem_limit_bytes=20 * 2**20),
        cost_estimate=brief,
    )(places, *[in_vmem(v) for v in parts], in_hbm(der), in_hbm(w), *[in_hbm(v) for _, v in held])


def column_tile(width):
    return next(t for t in (1024, 512, 256, 128, width) if width % t == 0)


def slice_kernel(place, x, w, term, piece):
    value = w[...]
    piece[...] = value
    product = lax.dot_general(value, x[...], (((0,), (1,)), ((), ())), preferred_element_type=f32)
    term[...] = product.T.astype(bf16)


def slice_call(place, x, w, width):
    rows, depth = x.shape
    tile = column_tile(width)
    steps = width // tile
    return pl.pallas_call(
        slice_kernel,
        grid_spec=pltpu.PrefetchScalarGridSpec(
            num_scalar_prefetch=1,
            grid=(steps,),
            in_specs=[
                pl.BlockSpec((rows, depth), lambda j, p: (0, 0)),
                pl.BlockSpec((depth, tile), lambda j, p: (0, p[2] * steps + j)),
            ],
            out_specs=[
                pl.BlockSpec((rows, tile), lambda j, p: (0, j)),
                pl.BlockSpec((depth, tile), lambda j, p: (0, j)),
            ],
        ),
        out_shape=[
            jax.ShapeDtypeStruct((rows, width), bf16),
            pltpu.HBM((depth, width), bf16),
        ],
        compiler_params=pltpu.CompilerParams(vmem_limit_bytes=16 * 2**20),
        cost_estimate=brief,
    )(place, x, in_hbm(w))


def pair_kernel(places, x_a, x_b, w, a, b):
    x = jnp.concatenate([x_a[...], x_b[...]], axis=0)
    product = lax.dot_general(w[...], x, (((0,), (1,)), ((), ())), preferred_element_type=f32)
    both = product.T.astype(bf16)
    rows = x_a.shape[0]
    a[...] = both[:rows]
    b[...] = both[rows:]


def pair_call(places, at, side, x, w, rows):
    depth, width = w.shape
    tile = column_tile(width)
    flat = pl.BlockSpec((rows, tile), lambda j, p: (0, j))
    return pl.pallas_call(
        pair_kernel,
        grid_spec=pltpu.PrefetchScalarGridSpec(
            num_scalar_prefetch=1,
            grid=(width // tile,),
            in_specs=[
                pl.BlockSpec((rows, depth), lambda j, p: (2 * p[at] + side, 0)),
                pl.BlockSpec((rows, depth), lambda j, p: (2 * p[at + 1] + side, 0)),
                pl.BlockSpec((depth, tile), lambda j, p: (0, j)),
            ],
            out_specs=[flat] * 2,
        ),
        out_shape=[pltpu.VMEM((rows, width), bf16)] * 2,
        compiler_params=pltpu.CompilerParams(vmem_limit_bytes=20 * 2**20),
        cost_estimate=brief,
    )(places, in_hbm(x), in_hbm(x), in_hbm(w))


def unset(shapes, kind=bf16):
    return pl.pallas_call(
        lambda *refs: None,
        out_specs=[pl.BlockSpec(memory_space=pltpu.HBM)] * len(shapes),
        out_shape=[pltpu.HBM(shape, kind) for shape in shapes],
        compiler_params=pltpu.CompilerParams(vmem_limit_bytes=2**20),
    )()


def body(tokens, w_up, w_down, cotangent):
    n_dp, n_col, n_row = (lax.axis_size(a) for a in ("dp", "col", "row"))
    n = n_dp * n_col
    rows, depth = tokens.shape
    grad_scale = float(rows * n) ** (-0.5)
    piece = w_up.shape[1] // n_dp
    dp, col, at = (lax.axis_index(a) for a in ("dp", "col", "row"))
    me = dp * n_col + col
    end = (at == 0) | (at == n_row - 1)
    def block(k, j):
        return (dp ^ k) * n_col + (col ^ j)

    def to_chip(value, k):
        return lax.ppermute(value, "dp", [(i, i ^ k) for i in range(n_dp)])

    def to_beside(value):
        return lax.ppermute(value, "col", [(0, 1), (1, 0)])

    outer = [(0, 1), (1, 0), (3, 2), (2, 3)]
    inner = [(1, 2), (2, 1)]

    chips = list(range(n_dp - 1, 0, -1))
    order = [("h", 0, 0), ("h", 0, 1), ("b", 0, 1)]
    order += [(kind, k, j) for kind in "hb" for k in chips for j in (0, 1)] + [("b", 0, 0)]
    total = len(order)
    forward_done = order.index(("h", chips[-1], 1)) + 3
    last = total + 2
    named = 3
    places = [end, me, dp] + [block(k, j) for _, k, j in order]
    places = jnp.stack([x.astype(jnp.int32) for x in places])
    places, end, col, tokens, cotangent = tie(places, end, col, tokens, cotangent)
    ahead = order.index(("b", chips[0], 0))
    pairs = {v - 1: v for v in range(3, ahead, 2)}
    for v in range(ahead, total - 1, 2):
        pairs[next(t for t in range(ahead - 2, total) if t not in pairs)] = v

    beside_t = to_beside(tokens)
    first_term, own_up = slice_call(places, tokens, w_up, piece)
    both_all = lax.all_gather(jnp.concatenate([tokens, cotangent]), ("dp", "col"), axis=0, tiled=True)
    beside_g = to_beside(cotangent)
    g_pair = jnp.concatenate([cotangent, beside_g])
    g_terms = lax.cond(
        col == 1,
        lambda p, x, w, y, v: (*slice_call(p, x, w, piece), times(y, v).astype(bf16)),
        lambda p, x, w, y, v: tuple(unset([(n_col * rows, piece), (depth, piece), (rows, piece)])),
        places,
        g_pair,
        w_down,
        beside_t,
        own_up,
    )

    term, first, middle = {0: first_term}, {}, {}
    whole, landed, own = {}, {}, {}
    state = {}
    e = None
    for t in range(total + 3):
        heads = {}
        if t < 2:
            heads["e_in"] = term[t]
        elif t < total + 2:
            heads["e_in"] = (middle[t - 2].astype(f32) + term[t - 2].astype(f32)).astype(bf16)
            if t < total:
                heads["e_in"] = jnp.where(end, term[t], heads["e_in"])
        if 1 <= t <= total:
            heads["m_in"] = (first[t - 1].astype(f32) + term[t - 1].astype(f32)).astype(bf16)
        if e is not None:
            heads["third"] = e
        if t == 0:
            heads.update({("g_terms", i): x for i, x in enumerate(g_terms)})
        if t == 1:
            heads["g_pair"] = g_pair
        if t >= 1:
            heads["own_up"] = own_up
            heads["tokens"] = tokens
            heads["cotangent"] = cotangent
            heads.update({("state", k): v for k, v in state.items()})
            heads.update({("whole", k): v for k, v in whole.items()})
        if t == last:
            heads.update({("landed", k): v[1] for k, v in landed.items()})
        heads = dict(zip(heads, tie(*heads.values())))
        if t == last:
            landed = {k: (-1, heads["landed", k]) for k in landed}
        own_up = heads.get("own_up", own_up)
        tokens, cotangent = heads.get("tokens", tokens), heads.get("cotangent", cotangent)
        state = {k: heads["state", k] for k in state}
        whole = {k: heads["whole", k] for k in whole}
        if t == 0:
            g_terms = [heads["g_terms", i] for i in range(3)]
        third = heads.get("third")
        fresh = {}
        if "e_in" in heads:
            fresh["e"] = lax.ppermute(heads["e_in"], "row", outer)
        if "m_in" in heads:
            fresh["m"] = lax.ppermute(heads["m_in"], "row", inner)
        if t == 0:
            term[1] = lax.cond(
                col == 1,
                lambda y, v, done: done,
                lambda y, v, done: times(y, v).astype(bf16),
                beside_t,
                own_up,
                g_terms[2],
            )
            fresh["term", 1] = term[1]
        if t == 1:
            both, own_down = lax.cond(
                col == 1,
                lambda p, x, w, done: tuple(done),
                lambda p, x, w, done: tuple(slice_call(p, x, w, piece)),
                places,
                heads["g_pair"],
                w_down,
                g_terms[:2],
            )
            term[2], own_last = both[rows:], both[:rows]
            whole["down"] = own_down
            fresh["whole", "down"] = own_down
            fresh["term", 2] = term[2]
            fresh["term", total - 1] = own_last
        if t in (4, 10):
            parted = whole["both"].reshape(n, 2, rows, depth)
            name, side = ("tokens_t", 0) if t == 4 else ("grads_t", 1)
            fresh["whole", name] = parted[:, side].reshape(n * rows, depth).T
        u = t - 3
        if u >= 0:
            kind, k, j = order[u]
            parts = [term[u], first[u], middle[u], third]
            if kind == "h":
                held = [state["act"], state["der"]] if "act" in state else []
                state["act"], state["der"] = forward_call(places, named + u, parts, held, (n * rows, piece))
            else:
                single = k in (0, chips[-1])
                state["grad"], part = backward_call(
                    places,
                    named + u,
                    parts,
                    state["der"],
                    own_up,
                    state.get("grad"),
                    whole.pop("pack", None),
                    None if single else j,
                    f32 if k == 0 else bf16,
                )
                if k == 0:
                    fresh["own", j] = part
                elif single and j == 1:
                    landed[k, j] = (last, to_chip(part, k))
                elif single:
                    fresh["send", (k, j)] = part
                elif j == 0:
                    fresh["whole", "pack"] = part
                else:
                    fresh["send", (k, None)] = part
        n_half = n * rows // 2
        if t in (forward_done, forward_done + 1):
            at_row = (t - forward_done) * n_half
            part = times_transposed(state["act"][at_row : at_row + n_half], whole["down"]).astype(bf16)
            out_part = whole.pop("out", None)
            if out_part is None:
                (out_part,) = unset([(n * rows, depth)])
            key = ("whole", "out") if at_row == 0 else ("out", 0)
            fresh[key] = lax.dynamic_update_slice(out_part, part, (at_row, 0))
        if t in (forward_done + 3, last - 1):
            at_row = 0 if t == forward_done + 3 else depth // 2
            part = grad_scale * times(whole["grads_t"][at_row : at_row + depth // 2], state["act"])
            down_grad = whole.get("down_grad")
            if down_grad is None:
                (down_grad,) = unset([(depth, piece)], f32)
            fresh["whole", "down_grad"] = lax.dynamic_update_slice(down_grad, part, (at_row, 0))
        if t in pairs:
            v = pairs[t]
            kind, k, j = order[v]
            side, w = (0, own_up) if kind == "h" else (1, whole["down"])
            both = whole.get("both", both_all)
            term[v], term[v + 1] = pair_call(places, named + v, side, both, w, rows)
            if "both" not in whole:
                fresh["whole", "both"] = both
            fresh["term", v], fresh["term", v + 1] = term[v], term[v + 1]
        for key in [key for key in landed if landed[key][0] == t]:
            fresh["landed", key] = landed[key][1]
        fresh.update({("state", k): x for k, x in state.items()})
        fresh = dict(zip(fresh, tie(*fresh.values())))
        e = fresh.get("e")
        if e is not None:
            first[t] = e
        if "m" in fresh:
            middle[t - 1] = fresh["m"]
        for key, x in fresh.items():
            if not isinstance(key, tuple):
                continue
            store, k = key
            if store == "landed":
                landed[k] = (-1, x)
            elif store == "send":
                landed[k] = (min(t + 3, last - 1), to_chip(x, k[0]))
            elif store == "out":
                output = lax.psum_scatter(x, ("dp", "col"), scatter_dimension=0, tiled=True)
            else:
                {"term": term, "whole": whole, "state": state, "own": own}[store][k] = x
    sums = [own[0], own[1]]
    for k, side in landed:
        part = landed[k, side][1].astype(f32)
        for j in (0, 1):
            if side is None:
                sums[j] = sums[j] + part[j * rows : (j + 1) * rows]
            elif side == j:
                sums[j] = sums[j] + part
    input_grad = sums[0] + to_beside(sums[1].astype(bf16)).astype(f32)
    up_grad = grad_scale * times(whole["tokens_t"], state["grad"])
    return (output, input_grad.astype(bf16), up_grad, whole["down_grad"])


def solution(mesh):
    placed = (P(("dp", "col"), "row"), P("row", "col"), P("row", "col"), P(("dp", "col"), "row"))
    return jax.shard_map(
        body,
        mesh=mesh,
        in_specs=placed,
        out_specs=(
            P(("dp", "col"), "row"),
            P(("dp", "col"), "row"),
            P("row", ("col", "dp")),
            P("row", ("col", "dp")),
        ),
        check_vma=False,
    )
```

```python
import functools

import jax
import jax.numpy as jnp
from jax import lax
from jax.experimental import pallas as pl
from jax.experimental.pallas import tpu as pltpu
from jax.sharding import PartitionSpec as P

gelu_coef = 0.7978845608
cubic_coef = 0.044715
bf16 = jnp.bfloat16
f32 = jnp.float32


def gelu_pair(hidden):
    tangent = jnp.tanh(gelu_coef * (hidden + cubic_coef * hidden * hidden * hidden))
    activated = 0.5 * hidden * (1.0 + tangent)
    derivative = 0.5 * (1.0 + tangent) + 0.5 * hidden * (1.0 - tangent * tangent) * gelu_coef * (
        1.0 + 3.0 * cubic_coef * hidden * hidden
    )
    return (activated, derivative)


def times(left, right):
    return jnp.dot(left, right, preferred_element_type=f32)


def times_transposed(left, right):
    return lax.dot_general(left, right, (((1,), (1,)), ((), ())), preferred_element_type=f32)


brief = pl.CostEstimate(flops=1, bytes_accessed=1, transcendentals=0)


def tie(*values):
    return lax.optimization_barrier(values)


def total_of(end, term, first, middle, third):
    inside = first[...].astype(f32) + middle[...].astype(f32)
    return term[...].astype(f32) + jnp.where(end, third[...].astype(f32), inside)


def in_hbm(value):
    return pltpu.with_memory_space_constraint(value, pltpu.HBM)


def in_vmem(value):
    return pltpu.with_memory_space_constraint(value, pltpu.VMEM)


def put_blocks(index, pairs, sems):
    copies = []
    for k, (tile, whole) in enumerate(pairs):
        rows = tile.shape[0]
        start = pl.multiple_of(index * rows, rows)
        copies.append(pltpu.make_async_copy(tile, whole.at[pl.ds(start, rows)], sems.at[k]))
    for copy in copies:
        copy.start()
    for copy in copies:
        copy.wait()


def forward_kernel(at, places, term, first, middle, third, *refs):
    act, der, act_tile, der_tile, sems = refs[-5:]
    hidden = total_of(places[0] == 1, term, first, middle, third)
    activated, derivative = gelu_pair(hidden)
    act_tile[...] = activated.astype(bf16)
    der_tile[...] = derivative.astype(bf16)
    put_blocks(places[at], [(act_tile, act), (der_tile, der)], sems)


def backward_kernel(at, places, term, first, middle, third, der, w, *refs):
    grad, part, block, sems = refs[-4:]
    rows = block.shape[0]
    start = pl.multiple_of(places[at] * rows, rows)
    save = pltpu.make_async_copy(block, grad.at[pl.ds(start, rows)], sems.at[0])
    step = pl.program_id(0)

    @pl.when(step == 0)
    def _():
        back = total_of(places[0] == 1, term, first, middle, third)
        block[...] = (back * der[...].astype(f32)).astype(bf16)
        save.start()

    product = lax.dot_general(w[...], block[...], (((1,), (1,)), ((), ())), preferred_element_type=f32)
    part[...] = product.T.astype(part.dtype)

    @pl.when(step == pl.num_programs(0) - 1)
    def _():
        save.wait()


def forward_call(places, at, parts, held, shape):
    rows, width = parts[0].shape
    plain = pl.BlockSpec((rows, width), lambda j, p: (0, 0))
    whole = pl.BlockSpec(memory_space=pltpu.HBM)
    return pl.pallas_call(
        functools.partial(forward_kernel, at),
        grid_spec=pltpu.PrefetchScalarGridSpec(
            num_scalar_prefetch=1,
            grid=(1,),
            in_specs=[plain] * 4 + [whole] * len(held),
            out_specs=[whole] * 2,
            scratch_shapes=[pltpu.VMEM((rows, width), bf16)] * 2 + [pltpu.SemaphoreType.DMA((2,))],
        ),
        out_shape=[pltpu.HBM(shape, bf16)] * 2,
        input_output_aliases={5 + k: k for k in range(len(held))},
        compiler_params=pltpu.CompilerParams(vmem_limit_bytes=16 * 2**20),
        cost_estimate=brief,
    )(places, *[in_vmem(v) for v in parts], *[in_hbm(v) for v in held])


def backward_call(places, at, parts, der, w, grad, pack, side, kind):
    rows, width = parts[0].shape
    depth = w.shape[0]
    held = [(k, v) for k, v in ((0, grad), (1, pack)) if v is not None]
    tile = column_tile(depth) // 2
    plain = pl.BlockSpec((rows, width), lambda j, p: (0, 0))
    whole = pl.BlockSpec(memory_space=pltpu.HBM)
    return pl.pallas_call(
        functools.partial(backward_kernel, at),
        grid_spec=pltpu.PrefetchScalarGridSpec(
            num_scalar_prefetch=1,
            grid=(depth // tile,),
            in_specs=[plain] * 4
            + [
                pl.BlockSpec((rows, width), lambda j, p: (p[at], 0)),
                pl.BlockSpec((tile, width), lambda j, p: (j, 0)),
            ]
            + [whole] * len(held),
            out_specs=[whole, pl.BlockSpec((rows, tile), lambda j, p: (side if pack is not None else 0, j))],
            scratch_shapes=[pltpu.VMEM((rows, width), bf16), pltpu.SemaphoreType.DMA((1,))],
        ),
        out_shape=[
            pltpu.HBM(der.shape, bf16),
            jax.ShapeDtypeStruct((2 * rows if side is not None else rows, depth), kind),
        ],
        input_output_aliases={7 + i: k for i, (k, _) in enumerate(held)},
        compiler_params=pltpu.CompilerParams(vmem_limit_bytes=20 * 2**20),
        cost_estimate=brief,
    )(places, *[in_vmem(v) for v in parts], in_hbm(der), in_hbm(w), *[in_hbm(v) for _, v in held])


def column_tile(width):
    return next(t for t in (1024, 512, 256, 128, width) if width % t == 0)


def slice_kernel(place, x, w, term, piece):
    value = w[...]
    piece[...] = value
    product = lax.dot_general(value, x[...], (((0,), (1,)), ((), ())), preferred_element_type=f32)
    term[...] = product.T.astype(bf16)


def slice_call(place, x, w, width):
    rows, depth = x.shape
    tile = column_tile(width)
    steps = width // tile
    return pl.pallas_call(
        slice_kernel,
        grid_spec=pltpu.PrefetchScalarGridSpec(
            num_scalar_prefetch=1,
            grid=(steps,),
            in_specs=[
                pl.BlockSpec((rows, depth), lambda j, p: (0, 0)),
                pl.BlockSpec((depth, tile), lambda j, p: (0, p[2] * steps + j)),
            ],
            out_specs=[
                pl.BlockSpec((rows, tile), lambda j, p: (0, j)),
                pl.BlockSpec((depth, tile), lambda j, p: (0, j)),
            ],
        ),
        out_shape=[
            jax.ShapeDtypeStruct((rows, width), bf16),
            pltpu.HBM((depth, width), bf16),
        ],
        compiler_params=pltpu.CompilerParams(vmem_limit_bytes=16 * 2**20),
        cost_estimate=brief,
    )(place, x, in_hbm(w))


def pair_kernel(places, x_a, x_b, w, a, b):
    x = jnp.concatenate([x_a[...], x_b[...]], axis=0)
    product = lax.dot_general(w[...], x, (((0,), (1,)), ((), ())), preferred_element_type=f32)
    both = product.T.astype(bf16)
    rows = x_a.shape[0]
    a[...] = both[:rows]
    b[...] = both[rows:]


def pair_call(places, at, side, x, w, rows):
    depth, width = w.shape
    tile = column_tile(width)
    flat = pl.BlockSpec((rows, tile), lambda j, p: (0, j))
    return pl.pallas_call(
        pair_kernel,
        grid_spec=pltpu.PrefetchScalarGridSpec(
            num_scalar_prefetch=1,
            grid=(width // tile,),
            in_specs=[
                pl.BlockSpec((rows, depth), lambda j, p: (2 * p[at] + side, 0)),
                pl.BlockSpec((rows, depth), lambda j, p: (2 * p[at + 1] + side, 0)),
                pl.BlockSpec((depth, tile), lambda j, p: (0, j)),
            ],
            out_specs=[flat] * 2,
        ),
        out_shape=[pltpu.VMEM((rows, width), bf16)] * 2,
        compiler_params=pltpu.CompilerParams(vmem_limit_bytes=20 * 2**20),
        cost_estimate=brief,
    )(places, in_hbm(x), in_hbm(x), in_hbm(w))


def unset(shapes, kind=bf16):
    return pl.pallas_call(
        lambda *refs: None,
        out_specs=[pl.BlockSpec(memory_space=pltpu.HBM)] * len(shapes),
        out_shape=[pltpu.HBM(shape, kind) for shape in shapes],
        compiler_params=pltpu.CompilerParams(vmem_limit_bytes=2**20),
    )()


def body(tokens, w_up, w_down, cotangent):
    n_dp, n_col, n_row = (lax.axis_size(a) for a in ("dp", "col", "row"))
    n = n_dp * n_col
    rows, depth = tokens.shape
    grad_scale = float(rows * n) ** (-0.5)
    piece = w_up.shape[1] // n_dp
    dp, col, at = (lax.axis_index(a) for a in ("dp", "col", "row"))
    me = dp * n_col + col
    end = (at == 0) | (at == n_row - 1)
    def block(k, j):
        return (dp ^ k) * n_col + (col ^ j)

    def to_chip(value, k):
        return lax.ppermute(value, "dp", [(i, i ^ k) for i in range(n_dp)])

    def to_beside(value):
        return lax.ppermute(value, "col", [(0, 1), (1, 0)])

    outer = [(0, 1), (1, 0), (3, 2), (2, 3)]
    inner = [(1, 2), (2, 1)]

    chips = list(range(n_dp - 1, 0, -1))
    order = [("h", 0, 0), ("h", 0, 1), ("b", 0, 1)]
    order += [(kind, k, j) for kind in "hb" for k in chips for j in (0, 1)] + [("b", 0, 0)]
    total = len(order)
    forward_done = order.index(("h", chips[-1], 1)) + 3
    last = total + 2
    named = 3
    places = [end, me, dp] + [block(k, j) for _, k, j in order]
    places = jnp.stack([x.astype(jnp.int32) for x in places])
    places, end, col, tokens, cotangent = tie(places, end, col, tokens, cotangent)
    ahead = order.index(("b", chips[0], 0))
    pairs = {v - 1: v for v in range(3, ahead, 2)}
    for v in range(ahead, total - 1, 2):
        pairs[next(t for t in range(ahead - 2, total) if t not in pairs)] = v

    beside_t = to_beside(tokens)
    first_term, own_up = slice_call(places, tokens, w_up, piece)
    both_all = lax.all_gather(jnp.concatenate([tokens, cotangent]), ("dp", "col"), axis=0, tiled=True)
    beside_g = to_beside(cotangent)
    second_term = lax.cond(
        col == 0,
        lambda y, v: times(y, v).astype(bf16),
        lambda y, v: unset([(rows, piece)])[0],
        beside_t,
        own_up,
    )

    term, first, middle = {0: first_term}, {}, {}
    whole, landed, own = {}, {}, {}
    state = {}
    e = None
    token = cotangent[: min(rows, 64)]
    for t in range(total + 3):
        heads = {}
        if t < 2:
            heads["e_in"] = term[t]
        elif t < total + 2:
            heads["e_in"] = (middle[t - 2].astype(f32) + term[t - 2].astype(f32)).astype(bf16)
            if t < total:
                heads["e_in"] = jnp.where(end, term[t], heads["e_in"])
        if 1 <= t <= total:
            heads["m_in"] = (first[t - 1].astype(f32) + term[t - 1].astype(f32)).astype(bf16)
        if e is not None:
            heads["third"] = e
        if t == 0:
            heads["second_term"] = second_term
        if t == 1:
            heads["g_pair"] = jnp.concatenate([cotangent, beside_g])
        heads["token"] = token
        if t >= 1:
            heads["own_up"] = own_up
            heads["tokens"] = tokens
            heads["cotangent"] = cotangent
            heads.update({("state", k): v for k, v in state.items()})
            heads.update({("whole", k): v for k, v in whole.items()})
        if t == last:
            heads["output"] = output
        heads = dict(zip(heads, tie(*heads.values())))
        output = heads.get("output", output if t > forward_done + 1 else None)
        own_up = heads.get("own_up", own_up)
        tokens, cotangent = heads.get("tokens", tokens), heads.get("cotangent", cotangent)
        state = {k: heads["state", k] for k in state}
        whole = {k: heads["whole", k] for k in whole}
        third = heads.get("third")
        token = heads["token"]
        fresh = {}
        if "e_in" in heads:
            fresh["e"] = lax.ppermute(heads["e_in"], "row", outer)
        if "m_in" in heads:
            fresh["m"] = lax.ppermute(heads["m_in"], "row", inner)
        if t == 0:
            term[1] = lax.cond(
                col == 0,
                lambda y, v, done: done,
                lambda y, v, done: times(y, v).astype(bf16),
                beside_t,
                own_up,
                heads["second_term"],
            )
            fresh["term", 1] = term[1]
        if t == 1:
            both, own_down = slice_call(places, heads["g_pair"], w_down, piece)
            term[2], own_last = both[rows:], both[:rows]
            whole["down"] = own_down
            fresh["whole", "down"] = own_down
            fresh["term", 2] = term[2]
            fresh["term", total - 1] = own_last
        if t in (4, 10):
            parted = whole["both"].reshape(n, 2, rows, depth)
            name, side = ("tokens_t", 0) if t == 4 else ("grads_t", 1)
            fresh["whole", name] = parted[:, side].reshape(n * rows, depth).T
        u = t - 3
        if u >= 0:
            kind, k, j = order[u]
            parts = [term[u], first[u], middle[u], third]
            if kind == "h":
                held = [state["act"], state["der"]] if "act" in state else []
                state["act"], state["der"] = forward_call(places, named + u, parts, held, (n * rows, piece))
            else:
                single = k in (0, chips[-1])
                state["grad"], part = backward_call(
                    places,
                    named + u,
                    parts,
                    state["der"],
                    own_up,
                    state.get("grad"),
                    whole.pop("pack", None),
                    None if single else j,
                    f32 if k == 0 else bf16,
                )
                if k == 0:
                    fresh["own", j] = part
                elif single and j == 1:
                    landed[k, j] = (last, to_chip(part, k))
                elif single:
                    fresh["send", (k, j)] = part
                elif j == 0:
                    fresh["whole", "pack"] = part
                else:
                    fresh["send", (k, None)] = part
        if 1 <= t <= forward_done - 2:
            token = lax.ppermute(heads["token"], "col", [(0, 1)])
            first_work = {("state", k): x for k, x in state.items()}
            first_work.update({k: x for k, x in fresh.items() if isinstance(k, tuple)})
            values = tie(token, *first_work.values(), *whole.values())
            token = values[0]
            for (store, k), x in zip(first_work, values[1:]):
                if store == "state":
                    state[k] = x
                elif store == "term":
                    term[k] = x
                if (store, k) in fresh:
                    fresh[store, k] = x
            whole = dict(zip(whole, values[1 + len(first_work) :]))
        n_half = n * rows // 2
        if t in (forward_done, forward_done + 1):
            at_row = (t - forward_done) * n_half
            part = times_transposed(state["act"][at_row : at_row + n_half], whole["down"]).astype(bf16)
            out_part = whole.pop("out", None)
            if out_part is None:
                (out_part,) = unset([(n * rows, depth)])
            key = ("whole", "out") if at_row == 0 else ("out", 0)
            fresh[key] = lax.dynamic_update_slice(out_part, part, (at_row, 0))
        if t in (forward_done + 3, last - 2):
            at_row = 0 if t == forward_done + 3 else depth // 2
            part = grad_scale * times(whole["grads_t"][at_row : at_row + depth // 2], state["act"])
            down_grad = whole.get("down_grad")
            if down_grad is None:
                (down_grad,) = unset([(depth, piece)], f32)
            fresh["whole", "down_grad"] = lax.dynamic_update_slice(down_grad, part, (at_row, 0))
        if t in pairs:
            v = pairs[t]
            kind, k, j = order[v]
            side, w = (0, own_up) if kind == "h" else (1, whole["down"])
            both = whole.get("both", both_all)
            term[v], term[v + 1] = pair_call(places, named + v, side, both, w, rows)
            if "both" not in whole:
                fresh["whole", "both"] = both
            fresh["term", v], fresh["term", v + 1] = term[v], term[v + 1]
        for key in [key for key in landed if landed[key][0] == t]:
            fresh["landed", key] = landed[key][1]
        if t == forward_done - 1:
            fresh["whole", "nothing"] = 0.0 * heads["token"][:1, :1].astype(f32)
        fresh.update({("state", k): x for k, x in state.items()})
        fresh = dict(zip(fresh, tie(*fresh.values())))
        e = fresh.get("e")
        if e is not None:
            first[t] = e
        if "m" in fresh:
            middle[t - 1] = fresh["m"]
        for key, x in fresh.items():
            if not isinstance(key, tuple):
                continue
            store, k = key
            if store == "landed":
                landed[k] = (-1, x)
            elif store == "send":
                landed[k] = (min(t + 3, last - 1), to_chip(x, k[0]))
            elif store == "out":
                output = lax.psum_scatter(x, ("dp", "col"), scatter_dimension=0, tiled=True)
            else:
                {"term": term, "whole": whole, "state": state, "own": own}[store][k] = x
    sums = [own[0], own[1]]
    for k, side in landed:
        part = landed[k, side][1]
        for j in (0, 1):
            if side is None:
                sums[j] = sums[j] + part[j * rows : (j + 1) * rows].astype(f32)
            elif side == j:
                sums[j] = sums[j] + part.astype(f32)
    input_grad = sums[0] + to_beside(sums[1].astype(bf16)).astype(f32)
    input_grad = input_grad + whole["nothing"]
    up_grad = grad_scale * times(whole["tokens_t"], state["grad"])
    return (output, input_grad.astype(bf16), up_grad, whole["down_grad"])


def solution(mesh):
    placed = (P(("dp", "col"), "row"), P("row", "col"), P("row", "col"), P(("dp", "col"), "row"))
    return jax.shard_map(
        body,
        mesh=mesh,
        in_specs=placed,
        out_specs=(
            P(("dp", "col"), "row"),
            P(("dp", "col"), "row"),
            P("row", ("col", "dp")),
            P("row", ("col", "dp")),
        ),
        check_vma=False,
    )
```

```python
import functools

import jax
import jax.numpy as jnp
from jax import lax
from jax.experimental import pallas as pl
from jax.experimental.pallas import tpu as pltpu
from jax.sharding import PartitionSpec as P

gelu_coef = 0.7978845608
cubic_coef = 0.044715
bf16 = jnp.bfloat16
f32 = jnp.float32


def gelu_pair(hidden):
    tangent = jnp.tanh(gelu_coef * (hidden + cubic_coef * hidden * hidden * hidden))
    activated = 0.5 * hidden * (1.0 + tangent)
    derivative = 0.5 * (1.0 + tangent) + 0.5 * hidden * (1.0 - tangent * tangent) * gelu_coef * (
        1.0 + 3.0 * cubic_coef * hidden * hidden
    )
    return (activated, derivative)


def times(left, right):
    return jnp.dot(left, right, preferred_element_type=f32)


def times_transposed(left, right):
    return lax.dot_general(left, right, (((1,), (1,)), ((), ())), preferred_element_type=f32)


brief = pl.CostEstimate(flops=1, bytes_accessed=1, transcendentals=0)


def tie(*values):
    return lax.optimization_barrier(values)


def total_of(end, term, first, middle, third):
    inside = first[...].astype(f32) + middle[...].astype(f32)
    return term[...].astype(f32) + jnp.where(end, third[...].astype(f32), inside)


def in_hbm(value):
    return pltpu.with_memory_space_constraint(value, pltpu.HBM)


def in_vmem(value):
    return pltpu.with_memory_space_constraint(value, pltpu.VMEM)


def put_blocks(index, pairs, sems):
    copies = []
    for k, (tile, whole) in enumerate(pairs):
        rows = tile.shape[0]
        start = pl.multiple_of(index * rows, rows)
        copies.append(pltpu.make_async_copy(tile, whole.at[pl.ds(start, rows)], sems.at[k]))
    for copy in copies:
        copy.start()
    for copy in copies:
        copy.wait()


def forward_kernel(at, places, term, first, middle, third, *refs):
    act, der, act_tile, der_tile, sems = refs[-5:]
    hidden = total_of(places[0] == 1, term, first, middle, third)
    activated, derivative = gelu_pair(hidden)
    act_tile[...] = activated.astype(bf16)
    der_tile[...] = derivative.astype(bf16)
    put_blocks(places[at], [(act_tile, act), (der_tile, der)], sems)


def backward_kernel(at, places, term, first, middle, third, der, w, *refs):
    grad, part, block, sems = refs[-4:]
    rows = block.shape[0]
    start = pl.multiple_of(places[at] * rows, rows)
    save = pltpu.make_async_copy(block, grad.at[pl.ds(start, rows)], sems.at[0])
    step = pl.program_id(0)

    @pl.when(step == 0)
    def _():
        back = total_of(places[0] == 1, term, first, middle, third)
        block[...] = (back * der[...].astype(f32)).astype(bf16)
        save.start()

    product = lax.dot_general(w[...], block[...], (((1,), (1,)), ((), ())), preferred_element_type=f32)
    part[...] = product.T.astype(part.dtype)

    @pl.when(step == pl.num_programs(0) - 1)
    def _():
        save.wait()


def forward_call(places, at, parts, held, shape):
    rows, width = parts[0].shape
    plain = pl.BlockSpec((rows, width), lambda j, p: (0, 0))
    whole = pl.BlockSpec(memory_space=pltpu.HBM)
    return pl.pallas_call(
        functools.partial(forward_kernel, at),
        grid_spec=pltpu.PrefetchScalarGridSpec(
            num_scalar_prefetch=1,
            grid=(1,),
            in_specs=[plain] * 4 + [whole] * len(held),
            out_specs=[whole] * 2,
            scratch_shapes=[pltpu.VMEM((rows, width), bf16)] * 2 + [pltpu.SemaphoreType.DMA((2,))],
        ),
        out_shape=[pltpu.HBM(shape, bf16)] * 2,
        input_output_aliases={5 + k: k for k in range(len(held))},
        compiler_params=pltpu.CompilerParams(vmem_limit_bytes=16 * 2**20),
        cost_estimate=brief,
    )(places, *[in_vmem(v) for v in parts], *[in_hbm(v) for v in held])


def backward_call(places, at, parts, der, w, grad, pack, side, kind):
    rows, width = parts[0].shape
    depth = w.shape[0]
    held = [(k, v) for k, v in ((0, grad), (1, pack)) if v is not None]
    tile = column_tile(depth) // 2
    plain = pl.BlockSpec((rows, width), lambda j, p: (0, 0))
    whole = pl.BlockSpec(memory_space=pltpu.HBM)
    return pl.pallas_call(
        functools.partial(backward_kernel, at),
        grid_spec=pltpu.PrefetchScalarGridSpec(
            num_scalar_prefetch=1,
            grid=(depth // tile,),
            in_specs=[plain] * 4
            + [
                pl.BlockSpec((rows, width), lambda j, p: (p[at], 0)),
                pl.BlockSpec((tile, width), lambda j, p: (j, 0)),
            ]
            + [whole] * len(held),
            out_specs=[whole, pl.BlockSpec((rows, tile), lambda j, p: (side if pack is not None else 0, j))],
            scratch_shapes=[pltpu.VMEM((rows, width), bf16), pltpu.SemaphoreType.DMA((1,))],
        ),
        out_shape=[
            pltpu.HBM(der.shape, bf16),
            jax.ShapeDtypeStruct((2 * rows if side is not None else rows, depth), kind),
        ],
        input_output_aliases={7 + i: k for i, (k, _) in enumerate(held)},
        compiler_params=pltpu.CompilerParams(vmem_limit_bytes=20 * 2**20),
        cost_estimate=brief,
    )(places, *[in_vmem(v) for v in parts], in_hbm(der), in_hbm(w), *[in_hbm(v) for _, v in held])


def column_tile(width):
    return next(t for t in (1024, 512, 256, 128, width) if width % t == 0)


def slice_kernel(place, x, w, term, piece):
    value = w[...]
    piece[...] = value
    product = lax.dot_general(value, x[...], (((0,), (1,)), ((), ())), preferred_element_type=f32)
    term[...] = product.T.astype(bf16)


def slice_call(place, x, w, width):
    rows, depth = x.shape
    tile = column_tile(width)
    steps = width // tile
    return pl.pallas_call(
        slice_kernel,
        grid_spec=pltpu.PrefetchScalarGridSpec(
            num_scalar_prefetch=1,
            grid=(steps,),
            in_specs=[
                pl.BlockSpec((rows, depth), lambda j, p: (0, 0)),
                pl.BlockSpec((depth, tile), lambda j, p: (0, p[2] * steps + j)),
            ],
            out_specs=[
                pl.BlockSpec((rows, tile), lambda j, p: (0, j)),
                pl.BlockSpec((depth, tile), lambda j, p: (0, j)),
            ],
        ),
        out_shape=[
            jax.ShapeDtypeStruct((rows, width), bf16),
            pltpu.HBM((depth, width), bf16),
        ],
        compiler_params=pltpu.CompilerParams(vmem_limit_bytes=16 * 2**20),
        cost_estimate=brief,
    )(place, x, in_hbm(w))


def pair_kernel(places, x_a, x_b, w, a, b):
    x = jnp.concatenate([x_a[...], x_b[...]], axis=0)
    product = lax.dot_general(w[...], x, (((0,), (1,)), ((), ())), preferred_element_type=f32)
    both = product.T.astype(bf16)
    rows = x_a.shape[0]
    a[...] = both[:rows]
    b[...] = both[rows:]


def pair_call(places, at, side, x, w, rows):
    depth, width = w.shape
    tile = column_tile(width)
    flat = pl.BlockSpec((rows, tile), lambda j, p: (0, j))
    return pl.pallas_call(
        pair_kernel,
        grid_spec=pltpu.PrefetchScalarGridSpec(
            num_scalar_prefetch=1,
            grid=(width // tile,),
            in_specs=[
                pl.BlockSpec((rows, depth), lambda j, p: (2 * p[at] + side, 0)),
                pl.BlockSpec((rows, depth), lambda j, p: (2 * p[at + 1] + side, 0)),
                pl.BlockSpec((depth, tile), lambda j, p: (0, j)),
            ],
            out_specs=[flat] * 2,
        ),
        out_shape=[pltpu.VMEM((rows, width), bf16)] * 2,
        compiler_params=pltpu.CompilerParams(vmem_limit_bytes=20 * 2**20),
        cost_estimate=brief,
    )(places, in_hbm(x), in_hbm(x), in_hbm(w))


def unset(shapes, kind=bf16):
    return pl.pallas_call(
        lambda *refs: None,
        out_specs=[pl.BlockSpec(memory_space=pltpu.HBM)] * len(shapes),
        out_shape=[pltpu.HBM(shape, kind) for shape in shapes],
        compiler_params=pltpu.CompilerParams(vmem_limit_bytes=2**20),
    )()


def body(tokens, w_up, w_down, cotangent):
    n_dp, n_col, n_row = (lax.axis_size(a) for a in ("dp", "col", "row"))
    n = n_dp * n_col
    rows, depth = tokens.shape
    grad_scale = float(rows * n) ** (-0.5)
    piece = w_up.shape[1] // n_dp
    dp, col, at = (lax.axis_index(a) for a in ("dp", "col", "row"))
    me = dp * n_col + col
    end = (at == 0) | (at == n_row - 1)
    def block(k, j):
        return (dp ^ k) * n_col + (col ^ j)

    def to_chip(value, k):
        return lax.ppermute(value, "dp", [(i, i ^ k) for i in range(n_dp)])

    def to_beside(value):
        return lax.ppermute(value, "col", [(0, 1), (1, 0)])

    outer = [(0, 1), (1, 0), (3, 2), (2, 3)]
    inner = [(1, 2), (2, 1)]

    chips = list(range(n_dp - 1, 0, -1))
    order = [("h", 0, 0), ("h", 0, 1), ("b", 0, 1)]
    order += [(kind, k, j) for kind in "hb" for k in chips for j in (0, 1)] + [("b", 0, 0)]
    total = len(order)
    forward_done = order.index(("h", chips[-1], 1)) + 3
    last = total + 2
    named = 3
    places = [end, me, dp] + [block(k, j) for _, k, j in order]
    places = jnp.stack([x.astype(jnp.int32) for x in places])
    places, end, col, tokens, cotangent = tie(places, end, col, tokens, cotangent)
    ahead = order.index(("b", chips[0], 0))
    pairs = {v - 1: v for v in range(3, ahead, 2)}
    for v in range(ahead, total - 1, 2):
        pairs[next(t for t in range(ahead - 2, total) if t not in pairs)] = v

    beside_t = to_beside(tokens)
    first_term, own_up = slice_call(places, tokens, w_up, piece)
    both_all = lax.all_gather(jnp.concatenate([tokens, cotangent]), ("dp", "col"), axis=0, tiled=True)
    beside_g = to_beside(cotangent)
    second_term = lax.cond(
        col == 0,
        lambda y, v: times(y, v).astype(bf16),
        lambda y, v: unset([(rows, piece)])[0],
        beside_t,
        own_up,
    )

    term, first, middle = {0: first_term}, {}, {}
    whole, landed, own = {}, {}, {}
    state = {}
    e = None
    token = cotangent[: min(rows, 64)]
    for t in range(total + 3):
        heads = {}
        if t < 2:
            heads["e_in"] = term[t]
        elif t < total + 2:
            heads["e_in"] = (middle[t - 2].astype(f32) + term[t - 2].astype(f32)).astype(bf16)
            if t < total:
                heads["e_in"] = jnp.where(end, term[t], heads["e_in"])
        if 1 <= t <= total:
            heads["m_in"] = (first[t - 1].astype(f32) + term[t - 1].astype(f32)).astype(bf16)
        if e is not None:
            heads["third"] = e
        if t == 0:
            heads["second_term"] = second_term
        if t == 1:
            heads["g_pair"] = jnp.concatenate([cotangent, beside_g])
        heads["token"] = token
        if t >= 1:
            heads["own_up"] = own_up
            heads["tokens"] = tokens
            heads["cotangent"] = cotangent
            heads.update({("state", k): v for k, v in state.items()})
            heads.update({("whole", k): v for k, v in whole.items()})
        if t == last:
            heads["output"] = output
        heads = dict(zip(heads, tie(*heads.values())))
        output = heads.get("output", output if t > forward_done + 1 else None)
        own_up = heads.get("own_up", own_up)
        tokens, cotangent = heads.get("tokens", tokens), heads.get("cotangent", cotangent)
        state = {k: heads["state", k] for k in state}
        whole = {k: heads["whole", k] for k in whole}
        third = heads.get("third")
        token = heads["token"]
        fresh = {}
        if "e_in" in heads:
            fresh["e"] = lax.ppermute(heads["e_in"], "row", outer)
        if "m_in" in heads:
            fresh["m"] = lax.ppermute(heads["m_in"], "row", inner)
        if t == 0:
            term[1] = lax.cond(
                col == 0,
                lambda y, v, done: done,
                lambda y, v, done: times(y, v).astype(bf16),
                beside_t,
                own_up,
                heads["second_term"],
            )
            fresh["term", 1] = term[1]
        if t == 1:
            both, own_down = slice_call(places, heads["g_pair"], w_down, piece)
            term[2], own_last = both[rows:], both[:rows]
            whole["down"] = own_down
            fresh["whole", "down"] = own_down
            fresh["term", 2] = term[2]
            fresh["term", total - 1] = own_last
        if t in (4, 10):
            parted = whole["both"].reshape(n, 2, rows, depth)
            name, side = ("tokens_t", 0) if t == 4 else ("grads_t", 1)
            fresh["whole", name] = parted[:, side].reshape(n * rows, depth).T
        u = t - 3
        if u >= 0:
            kind, k, j = order[u]
            parts = [term[u], first[u], middle[u], third]
            if kind == "h":
                held = [state["act"], state["der"]] if "act" in state else []
                state["act"], state["der"] = forward_call(places, named + u, parts, held, (n * rows, piece))
            else:
                single = k in (0, chips[-1])
                state["grad"], part = backward_call(
                    places,
                    named + u,
                    parts,
                    state["der"],
                    own_up,
                    state.get("grad"),
                    whole.pop("pack", None),
                    None if single else j,
                    f32 if k == 0 else bf16,
                )
                if k == 0:
                    fresh["own", j] = part
                elif single and j == 1:
                    landed[k, j] = (last, to_chip(part, k))
                elif single:
                    fresh["send", (k, j)] = part
                elif j == 0:
                    fresh["whole", "pack"] = part
                else:
                    fresh["send", (k, None)] = part
        if 3 <= t <= forward_done - 2:
            token = lax.ppermute(heads["token"], "col", [(0, 1)])
            first_work = {("state", k): x for k, x in state.items()}
            first_work.update({k: x for k, x in fresh.items() if isinstance(k, tuple)})
            values = tie(token, *first_work.values(), *whole.values())
            token = values[0]
            for (store, k), x in zip(first_work, values[1:]):
                if store == "state":
                    state[k] = x
                elif store == "term":
                    term[k] = x
                if (store, k) in fresh:
                    fresh[store, k] = x
            whole = dict(zip(whole, values[1 + len(first_work) :]))
        n_half = n * rows // 2
        if t in (forward_done, forward_done + 1):
            at_row = (t - forward_done) * n_half
            part = times_transposed(state["act"][at_row : at_row + n_half], whole["down"]).astype(bf16)
            out_part = whole.pop("out", None)
            if out_part is None:
                (out_part,) = unset([(n * rows, depth)])
            key = ("whole", "out") if at_row == 0 else ("out", 0)
            fresh[key] = lax.dynamic_update_slice(out_part, part, (at_row, 0))
        if t in (forward_done + 3, last - 2):
            at_row = 0 if t == forward_done + 3 else depth // 2
            part = grad_scale * times(whole["grads_t"][at_row : at_row + depth // 2], state["act"])
            down_grad = whole.get("down_grad")
            if down_grad is None:
                (down_grad,) = unset([(depth, piece)], f32)
            fresh["whole", "down_grad"] = lax.dynamic_update_slice(down_grad, part, (at_row, 0))
        if t in pairs:
            v = pairs[t]
            kind, k, j = order[v]
            side, w = (0, own_up) if kind == "h" else (1, whole["down"])
            both = whole.get("both", both_all)
            term[v], term[v + 1] = pair_call(places, named + v, side, both, w, rows)
            if "both" not in whole:
                fresh["whole", "both"] = both
            fresh["term", v], fresh["term", v + 1] = term[v], term[v + 1]
        for key in [key for key in landed if landed[key][0] == t]:
            fresh["landed", key] = landed[key][1]
        if t == forward_done - 1:
            fresh["whole", "nothing"] = 0.0 * heads["token"][:1, :1].astype(f32)
        fresh.update({("state", k): x for k, x in state.items()})
        fresh = dict(zip(fresh, tie(*fresh.values())))
        e = fresh.get("e")
        if e is not None:
            first[t] = e
        if "m" in fresh:
            middle[t - 1] = fresh["m"]
        for key, x in fresh.items():
            if not isinstance(key, tuple):
                continue
            store, k = key
            if store == "landed":
                landed[k] = (-1, x)
            elif store == "send":
                landed[k] = (min(t + 3, last - 1), to_chip(x, k[0]))
            elif store == "out":
                output = lax.psum_scatter(x, ("dp", "col"), scatter_dimension=0, tiled=True)
            else:
                {"term": term, "whole": whole, "state": state, "own": own}[store][k] = x
    sums = [own[0], own[1]]
    for k, side in landed:
        part = landed[k, side][1]
        for j in (0, 1):
            if side is None:
                sums[j] = sums[j] + part[j * rows : (j + 1) * rows].astype(f32)
            elif side == j:
                sums[j] = sums[j] + part.astype(f32)
    input_grad = sums[0] + to_beside(sums[1].astype(bf16)).astype(f32)
    input_grad = input_grad + whole["nothing"]
    up_grad = grad_scale * times(whole["tokens_t"], state["grad"])
    return (output, input_grad.astype(bf16), up_grad, whole["down_grad"])


def solution(mesh):
    placed = (P(("dp", "col"), "row"), P("row", "col"), P("row", "col"), P(("dp", "col"), "row"))
    return jax.shard_map(
        body,
        mesh=mesh,
        in_specs=placed,
        out_specs=(
            P(("dp", "col"), "row"),
            P(("dp", "col"), "row"),
            P("row", ("col", "dp")),
            P("row", ("col", "dp")),
        ),
        check_vma=False,
    )
```
